32 devices in a mesh: groups: 2 (over y), vocab: 4 (over z), tok: 2 (over x), sub: 2 (over core).
Axes of the slice: x: 2, y: 2, z: 4, core: 2. Of those that a mesh axis runs over, the one named last changes fastest.
Arguments:
- teacher_logits: bfloat16 [1024, 16384], P(('groups', 'tok', 'sub'), 'vocab'), parts along dimension 0, may hold values from -12 to 340
- student_logits: bfloat16 [1024, 256000], P(('groups', 'tok', 'sub'), 'vocab'), parts along dimension 0, may hold values from -12 to 340
- token_ids: int32 [1024], P(('groups', 'tok', 'sub')), parts along dimension 0, may hold values from 0 to 255999
- align_values: bfloat16 [128, 4096], P('vocab'), may hold values from 0.00049972534 to 0.049804688
- block_rows: int32 [128], P('vocab'), may hold values from 0 to 63
- block_cols: int32 [128], P('vocab'), may hold values from 0 to 999
- block_counts: int32 [4], P('vocab'), may hold values from 4 to 32, as said below
Outputs:
- logit_grad: bfloat16 [1024, 256000], P(('groups', 'tok', 'sub'), 'vocab'), parts along dimension 0
- token_loss: float32 [1024], P(('groups', 'tok', 'sub')), parts along dimension 0
The draws below stay inside these ranges and needn't reach their ends.
There are 2 independent parts, one for each index of `groups`. The reference program is written for one: setup_inputs(seed, part) draws one part's arguments, and reference() takes and returns one part's arrays. A program takes and returns all parts, laid end to end along the dimension named above; an argument that names none is the same for every part. Nothing has to cross between parts.
Inputs may be any that keep to these rules, and one draw needn't show every extreme that they name: Panel p uses its first block_counts[p] slots; later slots are not part of the alignment. Some panel uses all 32.
All inputs are finite; a program needn't handle non-finite values.
Results may differ from the reference program's by a relative error of at most 0.0034.
Values may be sent and summed in bfloat16 or wider, within the bound.
A program may use at most 256 MiB of HBM per device.

```python
import math
import jax
import jax.numpy as jnp
from jax import lax

VT_DEV = 4096
VS = 256000
BLK = 64
MAXB = 32
TOKENS = 512
VT = 16384
CB = 1000
PANELS = 4
SLOTS = 128
N_VOCAB = 4


def draw_teacher_logits(key, part):
    key = jax.random.fold_in(key, 11)
    table = jnp.clip(3.0 * jax.random.normal(key, (TOKENS, VT), jnp.float32), -12.0, 12.0)
    return table.astype(jnp.bfloat16)


def draw_student_logits(key, part):
    key = jax.random.fold_in(key, 12)
    table = jnp.clip(3.0 * jax.random.normal(key, (TOKENS, VS), jnp.float32), -12.0, 12.0)
    return table.astype(jnp.bfloat16)


def draw_block_counts(key, part):
    key = jax.random.fold_in(key, 13)
    key_shift, key_full = jax.random.split(key)
    shifts = jax.random.randint(key_shift, (PANELS,), 0, 4)
    counts = jnp.right_shift(jnp.full((PANELS,), MAXB, jnp.int32), shifts)
    full_panel = jax.random.randint(key_full, (), 0, PANELS)
    counts = counts.at[full_panel].set(MAXB)
    counts = counts.at[(full_panel + 1) % PANELS].set(MAXB // 8)
    return counts.astype(jnp.int32)


def place_ends(entries, key, smallest, top_value):
    spot = [jax.random.randint(jax.random.fold_in(key, axis), (), 0, length) for axis, length in enumerate(entries.shape)]
    main_axis = entries.shape.index(max(entries.shape))
    beside = spot[:main_axis] + [(spot[main_axis] + 1) % entries.shape[main_axis]] + spot[main_axis + 1:]
    return entries.at[tuple(spot)].set(smallest).at[tuple(beside)].set(top_value)


def level_of(rng, dims, cuts, least, high):
    level = 1.0
    for position, blocks in cuts:
        steps = jax.random.uniform(jax.random.fold_in(jax.random.fold_in(rng, 6), position), (blocks,), jnp.float32, least / len(cuts), high / len(cuts))
        level = level * jnp.repeat(jnp.exp(steps), dims[position] // blocks).reshape((-1,) + (1,) * (len(dims) - 1 - position))
    return level


def setup_inputs(seed: int = 0, part: int = 0) -> dict:
    arg_keys = jax.random.split(jax.random.key(seed), 8)
    part_splits = jax.random.split(jax.random.fold_in(arg_keys[7], part), 8)
    teacher_logits = draw_teacher_logits(jax.random.fold_in(jax.random.fold_in(arg_keys[7], part), 71), part)
    student_logits = draw_student_logits(jax.random.fold_in(jax.random.fold_in(arg_keys[7], part), 71), part)
    token_ids = place_ends(jax.random.randint(part_splits[2], (TOKENS,), 0, VS), jax.random.fold_in(part_splits[2], 1), 0, VS - 1).astype(jnp.int32)
    align_values = jnp.clip(jnp.exp(math.log(0.049804688) - 4.6018058 * jax.random.uniform(arg_keys[3], (SLOTS, BLK * BLK), jnp.float32) ** level_of(arg_keys[3], (SLOTS, BLK * BLK), ((0, 4),), -0.2, 0.2)), 0.00049972534, 0.049804688).astype(jnp.bfloat16)
    block_rows = place_ends(jax.random.randint(arg_keys[4], (SLOTS,), 0, VT_DEV // BLK), jax.random.fold_in(arg_keys[4], 1), 0, (VT_DEV // BLK) - 1).astype(jnp.int32)
    block_cols = place_ends(jax.random.randint(arg_keys[5], (SLOTS,), 0, CB), jax.random.fold_in(arg_keys[5], 1), 0, CB - 1).astype(jnp.int32)
    block_counts = draw_block_counts(jax.random.fold_in(arg_keys[7], 71), part)
    return {"teacher_logits": teacher_logits, "student_logits": student_logits, "token_ids": token_ids, "align_values": align_values, "block_rows": block_rows, "block_cols": block_cols, "block_counts": block_counts}


def alignment_blocks(align_values, block_rows, block_cols, block_counts):
    slot_ids = jnp.arange(N_VOCAB * MAXB, dtype=jnp.int32)
    owner_ids = slot_ids // MAXB
    inner_ids = slot_ids % MAXB
    live_slots = inner_ids < block_counts[owner_ids]
    dest_ids = inner_ids // (MAXB // N_VOCAB)
    row_ids = owner_ids * (VT_DEV // BLK) + block_rows
    col_ids = dest_ids * (VS // (N_VOCAB * BLK)) + block_cols
    masked = align_values * live_slots[:, None].astype(align_values.dtype)
    return row_ids, col_ids, masked.reshape(-1, BLK, BLK).astype(jnp.float32)


def reference(teacher_logits, student_logits, token_ids, align_values, block_rows, block_cols, block_counts):
    row_ids, col_ids, blocks = alignment_blocks(align_values, block_rows, block_cols, block_counts)
    group_count = 8
    teacher_groups = teacher_logits.reshape(group_count, -1, teacher_logits.shape[1])
    student_groups = student_logits.reshape(group_count, -1, student_logits.shape[1])
    id_groups = token_ids.reshape(group_count, -1)

    def one_group(inputs):
        teacher_part, student_part, id_part = inputs
        scores = teacher_part.astype(jnp.float32)
        row_top = jnp.max(scores, axis=1, keepdims=True)
        raised = jnp.exp(scores - row_top)
        teacher_probs = (raised / jnp.sum(raised, axis=1, keepdims=True)).astype(jnp.bfloat16)
        row_count = teacher_probs.shape[0]
        picked_cols = teacher_probs.reshape(row_count, -1, BLK)[:, row_ids, :].astype(jnp.float32)
        block_terms = jnp.einsum("tbk,bkc->btc", picked_cols, blocks)
        target = jnp.zeros((VS // BLK, row_count, BLK), jnp.float32).at[col_ids].add(block_terms)
        target = jnp.transpose(target, (1, 0, 2)).reshape(row_count, VS)
        logits = student_part.astype(jnp.float32)
        student_top = jnp.max(logits, axis=1)
        log_norm = student_top + jnp.log(jnp.sum(jnp.exp(logits - student_top[:, None]), axis=1))
        mass = jnp.sum(target, axis=1)
        cross = jnp.sum(target * logits, axis=1)
        id_hit = jnp.arange(VS, dtype=jnp.int32)[None, :] == id_part[:, None]
        picked = jnp.sum(jnp.where(id_hit, logits, jnp.zeros_like(logits)), axis=1)
        weight = mass + 1.0
        token_loss = weight * log_norm - cross - picked
        logit_grad = weight[:, None] * jnp.exp(logits - log_norm[:, None]) - target - id_hit.astype(jnp.float32)
        return logit_grad.astype(jnp.bfloat16), token_loss

    grads, losses = lax.map(one_group, (teacher_groups, student_groups, id_groups))
    return grads.reshape(TOKENS, VS), losses.reshape(TOKENS)
```

```python
import functools

import jax
import jax.numpy as jnp
from jax import lax
from jax.experimental import pallas as pl
from jax.experimental.pallas import tpu as pltpu
from jax.sharding import PartitionSpec as P

BLK = 64
MAXB = 32
LANES = 128
ROWS = 16
CHUNK = 1280
VMEM = pltpu.VMEM
SMEM = pltpu.SMEM
LIMIT = 40 * 1024 * 1024


def lane_tile(index):
    return pl.ds(pl.multiple_of(index * LANES, LANES), LANES)


def fold(value, join):
    parts = [value[:, k : k + LANES] for k in range(0, value.shape[1], LANES)]
    while len(parts) > 1:
        parts = [join(*parts[k : k + 2]) if k + 1 < len(parts) else parts[k] for k in range(0, len(parts), 2)]
    return parts[0]


def pick_kernel(rows_ref, logits_ref, top_ref, total_ref, picks_ref):
    top = top_ref[...]
    total = total_ref[...]

    def body(slot, _):
        row = rows_ref[slot]
        scores = logits_ref[:, lane_tile(row // 2)].astype(jnp.float32)
        probs = jnp.transpose(jnp.exp(scores - top) / total)
        picks_ref[slot] = jnp.where(row % 2 == 0, probs[:BLK], probs[BLK:]).astype(jnp.bfloat16)
        return _

    lax.fori_loop(0, MAXB, body, 0, unroll=4)


def stats_kernel(width, tile_ref, ids_ref, logits_ref, top_ref, total_ref, picked_ref, seen_ref):
    step = pl.program_id(0)
    whole = width // CHUNK
    tail = logits_ref.shape[1] - whole * CHUNK

    def chunk(index):
        return logits_ref[:, pl.ds(pl.multiple_of(index * CHUNK, CHUNK), CHUNK)]

    def max_body(index, top):
        return jnp.maximum(top, fold(chunk(index), jnp.maximum))

    top = lax.fori_loop(
        0, whole, max_body, jnp.full((ROWS, LANES), -jnp.inf, jnp.bfloat16), unroll=2
    ).astype(jnp.float32)
    if tail:
        rest = logits_ref[:, whole * CHUNK :].astype(jnp.float32)
        live = lax.broadcasted_iota(jnp.int32, rest.shape, 1) < width - whole * CHUNK
        top = jnp.maximum(top, fold(jnp.where(live, rest, -jnp.inf), jnp.maximum))
    top = jnp.max(top, axis=1, keepdims=True)

    def sum_body(index, total):
        return total + fold(jnp.exp(chunk(index).astype(jnp.float32) - top), jnp.add)

    total = lax.fori_loop(0, whole, sum_body, jnp.zeros((ROWS, LANES), jnp.float32), unroll=2)
    if tail:
        total = total + fold(jnp.where(live, jnp.exp(rest - top), 0.0), jnp.add)
    top_ref[...] = top
    total_ref[...] = jnp.sum(total, axis=1, keepdims=True)

    row_iota = lax.broadcasted_iota(jnp.int32, (ROWS, LANES), 0)
    lane_iota = lax.broadcasted_iota(jnp.int32, (ROWS, LANES), 1)
    picked = jnp.zeros((ROWS, LANES), jnp.float32)
    for row in range(ROWS):
        place = ids_ref[step * ROWS + row]
        tile = jnp.clip(place, 0, width - 1) // LANES
        here = logits_ref[:, lane_tile(tile)].astype(jnp.float32)
        hit = (row_iota == row) & (lane_iota == place - tile * LANES)
        picked = jnp.where(hit, here, picked)
    picked_ref[...] = jnp.sum(picked, axis=1, keepdims=True)
    for slot in range(MAXB):
        seen_ref[slot] = logits_ref[:, lane_tile(tile_ref[slot])]


def target_kernel(half_ref, first_ref, picks_ref, blocks_ref, seen_ref, target_ref, mass_ref, cross_ref):
    target_ref[...] = jnp.zeros_like(target_ref)
    rows = target_ref.shape[1]
    side = lax.broadcasted_iota(jnp.int32, (1, LANES), 1) // BLK

    def body(slot, carry):
        mass, cross = carry
        here = side == half_ref[slot]
        block = jnp.where(here, blocks_ref[slot].astype(jnp.float32), 0.0).astype(jnp.bfloat16)
        term = lax.dot_general(
            picks_ref[slot], block, (((0,), (0,)), ((), ())), preferred_element_type=jnp.float32
        )
        first = first_ref[slot]
        target_ref[first] = target_ref[first] + term
        return mass + term, cross + jnp.where(here, term * seen_ref[slot].astype(jnp.float32), 0.0)

    zero = jnp.zeros((rows, LANES), jnp.float32)
    mass, cross = lax.fori_loop(0, MAXB, body, (zero, zero), unroll=2)
    mass_ref[...] = jnp.sum(mass, axis=1, keepdims=True)
    cross_ref[...] = jnp.sum(cross, axis=1, keepdims=True)


def grad_kernel(tile_ref, first_ref, ids_ref, shift_ref, target_ref, logits_ref, grad_ref):
    width = logits_ref.shape[1]
    shift = shift_ref[...]
    ids = ids_ref[...]

    def part(start, size):
        scores = logits_ref[:, pl.ds(start, size)].astype(jnp.float32)
        hit = lax.broadcasted_iota(jnp.int32, (ROWS, size), 1) == ids - start
        return jnp.exp(scores - shift) - jnp.where(hit, 1.0, 0.0)

    def body(index, _):
        start = pl.multiple_of(index * CHUNK, CHUNK)
        grad_ref[:, pl.ds(start, CHUNK)] = part(start, CHUNK).astype(jnp.bfloat16)
        return _

    whole = width // CHUNK
    lax.fori_loop(0, whole, body, 0, unroll=2)
    if width % CHUNK:
        start = whole * CHUNK
        grad_ref[:, pl.ds(start, width - start)] = part(start, width - start).astype(jnp.bfloat16)
    for slot in range(MAXB):
        start = pl.multiple_of(tile_ref[slot] * LANES, LANES)
        grad = part(start, LANES) - target_ref[first_ref[slot]]
        grad_ref[:, pl.ds(start, LANES)] = grad.astype(jnp.bfloat16)


def params():
    return pltpu.CompilerParams(vmem_limit_bytes=LIMIT)


def local(
    teacher_logits, student_logits, token_ids, align_values, block_rows, block_cols, block_counts
):
    count = lax.axis_size("vocab")
    me = lax.axis_index("vocab")
    rows = teacher_logits.shape[0]
    width = student_logits.shape[1]
    padded = pl.cdiv(width, LANES) * LANES
    per_dest = MAXB // count
    steps = rows // ROWS
    smem = pl.BlockSpec(memory_space=SMEM)
    vmem = pl.BlockSpec(memory_space=VMEM)
    f32 = lambda *shape: jax.ShapeDtypeStruct(shape, jnp.float32)
    b16 = lambda *shape: jax.ShapeDtypeStruct(shape, jnp.bfloat16)

    live = lax.iota(jnp.int32, MAXB) < block_counts[0]
    sent_blocks = jnp.where(live[:, None], align_values, jnp.zeros_like(align_values))
    blocks = lax.all_to_all(sent_blocks, "vocab", split_axis=0, concat_axis=0, tiled=True)

    scores = teacher_logits.astype(jnp.float32)
    part_top = jnp.max(scores, axis=1)
    part_total = jnp.sum(jnp.exp(scores - part_top[:, None]), axis=1)
    parts = lax.all_gather(
        jnp.concatenate([part_top, part_total, block_cols.astype(jnp.float32)]), "vocab"
    )
    tops, totals = parts[:, :rows], parts[:, rows : 2 * rows]
    top = jnp.max(tops, axis=0)
    total = jnp.sum(totals * jnp.exp(tops - top), axis=0)
    cols = parts[:, 2 * rows :].astype(jnp.int32).reshape(count, count, per_dest)
    cols = lax.dynamic_index_in_dim(cols, me, 1, keepdims=False).reshape(MAXB)
    tile, half = cols // 2, cols % 2
    first = jnp.argmax(tile[:, None] == tile[None, :], axis=1).astype(jnp.int32)

    picks = pl.pallas_call(
        pick_kernel,
        out_shape=b16(MAXB, BLK, rows),
        in_specs=[smem, vmem, vmem, vmem],
        out_specs=vmem,
        compiler_params=params(),
    )(block_rows, teacher_logits, top[:, None], total[:, None])
    picks = lax.all_to_all(picks, "vocab", split_axis=0, concat_axis=0, tiled=True)

    ids = token_ids - me * width
    row_spec = pl.BlockSpec((ROWS, 1), lambda i: (i, 0))
    wide_spec = pl.BlockSpec((ROWS, padded), lambda i: (i, 0))
    slot_spec = pl.BlockSpec((MAXB, ROWS, LANES), lambda i: (0, i, 0))
    size = rows * width
    student_top, student_total, picked, seen = pl.pallas_call(
        functools.partial(stats_kernel, width),
        out_shape=(f32(rows, 1), f32(rows, 1), f32(rows, 1), b16(MAXB, rows, LANES)),
        grid=(steps,),
        in_specs=[smem, smem, wide_spec],
        out_specs=(row_spec, row_spec, row_spec, slot_spec),
        compiler_params=params(),
        cost_estimate=pl.CostEstimate(flops=8 * size, bytes_accessed=2 * size, transcendentals=size),
    )(tile, ids, student_logits)

    blocks = blocks.reshape(MAXB, BLK, BLK)
    blocks = jnp.concatenate([blocks, blocks], axis=2)
    target, mass, cross = pl.pallas_call(
        target_kernel,
        out_shape=(f32(MAXB, rows, LANES), f32(rows, 1), f32(rows, 1)),
        in_specs=[smem, smem, vmem, vmem, vmem],
        out_specs=(vmem, vmem, vmem),
        compiler_params=params(),
    )(half, first, picks, blocks, seen)

    sums = jnp.concatenate([student_top, student_total, mass, cross, picked], axis=1).T
    sums = lax.all_gather(sums, "vocab")
    top = jnp.max(sums[:, 0], axis=0)
    total = jnp.sum(sums[:, 1] * jnp.exp(sums[:, 0] - top), axis=0)
    mass, cross, picked = jnp.sum(sums[:, 2:], axis=0)
    log_norm = top + jnp.log(total)
    weight = mass + 1.0
    token_loss = weight * log_norm - cross - picked
    shift = log_norm - jnp.log(weight)

    logit_grad = pl.pallas_call(
        grad_kernel,
        out_shape=b16(rows, width),
        grid=(steps,),
        in_specs=[smem, smem, row_spec, row_spec, slot_spec, wide_spec],
        out_specs=wide_spec,
        compiler_params=params(),
        cost_estimate=pl.CostEstimate(flops=8 * size, bytes_accessed=4 * size, transcendentals=size),
    )(tile, first, ids[:, None], shift[:, None], target, student_logits)
    return logit_grad, token_loss


def solution(mesh):
    return jax.shard_map(
        local,
        mesh=mesh,
        in_specs=(
            P(("groups", "tok", "sub"), "vocab"),
            P(("groups", "tok", "sub"), "vocab"),
            P(("groups", "tok", "sub")),
            P("vocab", None),
            P("vocab"),
            P("vocab"),
            P("vocab"),
        ),
        out_specs=(P(("groups", "tok", "sub"), "vocab"), P(("groups", "tok", "sub"))),
        check_vma=False,
    )
```

```python
import functools

import jax
import jax.numpy as jnp
from jax import lax
from jax.experimental import pallas as pl
from jax.experimental.pallas import tpu as pltpu
from jax.sharding import PartitionSpec as P

BLK = 64
MAXB = 32
LANES = 128
ROWS = 16
CHUNK = 2560
VMEM = pltpu.VMEM
SMEM = pltpu.SMEM
LIMIT = 40 * 1024 * 1024


def lane_tile(index):
    return pl.ds(pl.multiple_of(index * LANES, LANES), LANES)


def fold(value, join):
    parts = [value[:, k : k + LANES] for k in range(0, value.shape[1], LANES)]
    while len(parts) > 1:
        parts = [join(*parts[k : k + 2]) if k + 1 < len(parts) else parts[k] for k in range(0, len(parts), 2)]
    return parts[0]


def row_stats(load, width):
    whole, tail = divmod(width, CHUNK)

    def chunk(index):
        return load(pl.multiple_of(index * CHUNK, CHUNK), CHUNK)

    def max_body(index, top):
        return jnp.maximum(top, fold(chunk(index), jnp.maximum))

    top = jnp.full((ROWS, LANES), -jnp.inf, jnp.bfloat16)
    top = lax.fori_loop(0, whole, max_body, top).astype(jnp.float32)
    top = jnp.max(top, axis=1, keepdims=True)
    if tail:
        rest = load(whole * CHUNK, tail).astype(jnp.float32)
        top = jnp.maximum(top, jnp.max(rest, axis=1, keepdims=True))

    def sum_body(index, total):
        return total + fold(jnp.exp(chunk(index).astype(jnp.float32) - top), jnp.add)

    total = lax.fori_loop(0, whole, sum_body, jnp.zeros((ROWS, LANES), jnp.float32))
    total = jnp.sum(total, axis=1, keepdims=True)
    if tail:
        total = total + jnp.sum(jnp.exp(rest - top), axis=1, keepdims=True)
    return top, total


def greet(others):
    barrier = pltpu.get_barrier_semaphore()
    for other in others:
        pl.semaphore_signal(
            barrier, inc=1, device_id={"vocab": other}, device_id_type=pl.DeviceIdType.MESH
        )
    return barrier


def remote(source, target, send_sem, recv_sem, other):
    return pltpu.make_async_remote_copy(
        src_ref=source,
        dst_ref=target,
        send_sem=send_sem,
        recv_sem=recv_sem,
        device_id={"vocab": other},
        device_id_type=pl.DeviceIdType.MESH,
    )


def rows_of(index):
    return pl.ds(pl.multiple_of(index * ROWS, ROWS), ROWS)


def spread(part):
    return jnp.broadcast_to(part, (part.shape[0], LANES))


def teacher_kernel(
    count, cols_ref, teacher_ref, stats_ref, all_cols_ref,
    top_at, total_at, own_stats, stats, cols, send_sem, recv_sem,
):
    me = lax.axis_index("vocab")
    others = [lax.rem(me + step, count) for step in range(1, count)]
    barrier = greet(others)

    def body(index, _):
        here = rows_of(index)
        top, total = row_stats(lambda start, size: teacher_ref[here, pl.ds(start, size)], teacher_ref.shape[1])
        top_at[here, :] = spread(top)
        total_at[here, :] = spread(total)
        return _

    lax.fori_loop(0, teacher_ref.shape[0] // ROWS, body, 0)
    sub_iota = lax.broadcasted_iota(jnp.int32, (8, LANES), 0)
    own_stats[...] = jnp.where(
        sub_iota == 0, jnp.transpose(top_at[...])[:8], jnp.transpose(total_at[...])[:8]
    )
    stats[me] = own_stats[...]
    cols[me] = cols_ref[...]
    pl.semaphore_wait(barrier, count - 1)
    copies = []
    for step, other in enumerate(others):
        copies.append(remote(own_stats, stats.at[me], send_sem.at[0, step], recv_sem.at[0, me], other))
        copies.append(remote(cols_ref, cols.at[me], send_sem.at[1, step], recv_sem.at[1, me], other))
    for copy in copies:
        copy.start()
    for step, other in enumerate(others):
        remote(own_stats, stats.at[other], send_sem.at[0, step], recv_sem.at[0, other], other).wait_recv()
        remote(cols_ref, cols.at[other], send_sem.at[1, step], recv_sem.at[1, other], other).wait_recv()
    tops = [stats[index, 0:1] for index in range(count)]
    totals = [stats[index, 1:2] for index in range(count)]
    top = functools.reduce(jnp.maximum, tops)
    total = sum(part * jnp.exp(peak - top) for part, peak in zip(totals, tops))
    stats_ref[...] = jnp.where(sub_iota == 0, top, total)
    all_cols_ref[...] = cols[...]
    for copy in copies:
        copy.wait_send()


def pick_kernel(
    rows_ref, tile_ref, ids_ref, place_ref, teacher_ref, stats_ref, student_ref,
    picks_ref, seen_ref, picked_ref, near, seen_sem, near_sem,
):
    tokens = teacher_ref.shape[0]

    def near_copy(token):
        return pltpu.make_async_copy(
            student_ref.at[rows_of(token // ROWS), lane_tile(place_ref[token])],
            near.at[token],
            near_sem.at[token],
        )

    def seen_copy(slot):
        return pltpu.make_async_copy(
            student_ref.at[:, lane_tile(tile_ref[slot])], seen_ref.at[slot], seen_sem.at[slot]
        )

    def start_near(token, _):
        near_copy(token).start()
        return _

    def start_seen(slot, _):
        seen_copy(slot).start()
        return _

    lax.fori_loop(0, tokens, start_near, 0, unroll=8)
    lax.fori_loop(0, MAXB, start_seen, 0, unroll=8)
    top = stats_ref[0:1]
    total = stats_ref[1:2]

    def body(slot, _):
        row = rows_ref[slot]
        scores = jnp.transpose(teacher_ref[:, lane_tile(row // 2)].astype(jnp.float32))
        scores = jnp.where(row % 2 == 0, scores[:BLK], scores[BLK:])
        picks_ref[slot] = (jnp.exp(scores - top) / total).astype(jnp.bfloat16)
        return _

    lax.fori_loop(0, MAXB, body, 0, unroll=4)

    row_iota = lax.broadcasted_iota(jnp.int32, (ROWS, LANES), 0)
    lane_iota = lax.broadcasted_iota(jnp.int32, (ROWS, LANES), 1)

    def picked_body(index, _):
        picked = jnp.zeros((ROWS, LANES), jnp.float32)
        for row in range(ROWS):
            token = index * ROWS + row
            near_copy(token).wait()
            hit = (row_iota == row) & (lane_iota == ids_ref[token] - place_ref[token] * LANES)
            picked = jnp.where(hit, near[token].astype(jnp.float32), picked)
        picked_ref[rows_of(index), :] = spread(jnp.sum(picked, axis=1, keepdims=True))
        return _

    lax.fori_loop(0, tokens // ROWS, picked_body, 0)

    def wait_seen(slot, _):
        seen_copy(slot).wait()
        return _

    lax.fori_loop(0, MAXB, wait_seen, 0, unroll=8)


def loss_kernel(
    count, sides_ref, picks_ref, blocks_ref, seen_ref, picked_ref, student_ref,
    target_ref, shift_ref, loss_ref,
    logits, top_at, total_at, own_sums, sums, picks, blocks, load_sem, send_sem, recv_sem,
):
    me = lax.axis_index("vocab")
    tokens, width = logits.shape
    per = MAXB // count
    others = [lax.rem(me + step, count) for step in range(1, count)]
    slots = lambda owner: pl.ds(owner * per, per)

    def load(index):
        return pltpu.make_async_copy(
            student_ref.at[rows_of(index)], logits.at[rows_of(index)], load_sem.at[index]
        )

    for index in range(tokens // ROWS):
        load(index).start()
    barrier = greet(others)
    for slot in range(per):
        blocks[me * per + slot] = blocks_ref[me * per + slot]
        picks[me * per + slot] = picks_ref[me * per + slot]
    pl.semaphore_wait(barrier, count - 1)
    copies = []
    for step, other in enumerate(others):
        for kind, source, buffer in ((0, picks_ref, picks), (1, blocks_ref, blocks)):
            copies.append(
                remote(
                    source.at[slots(other)], buffer.at[slots(me)],
                    send_sem.at[kind, step], recv_sem.at[kind, me], other,
                )
            )
    for copy in copies:
        copy.start()

    def student_body(index, _):
        load(index).wait()
        here = rows_of(index)
        top, total = row_stats(lambda start, size: logits[here, pl.ds(start, size)], width)
        top_at[here, :] = spread(top)
        total_at[here, :] = spread(total)
        return _

    lax.fori_loop(0, tokens // ROWS, student_body, 0)

    for step, other in enumerate(others):
        for kind, source, buffer in ((0, picks_ref, picks), (1, blocks_ref, blocks)):
            remote(
                source.at[slots(other)], buffer.at[slots(other)],
                send_sem.at[kind, step], recv_sem.at[kind, other], other,
            ).wait_recv()

    left = lax.broadcasted_iota(jnp.int32, (1, LANES), 1) < BLK

    def target_body(slot, carry):
        mass, cross = carry
        packed = blocks[slot].astype(jnp.float32)
        turned = pltpu.roll(packed, BLK, 1)
        block = jnp.concatenate(
            [jnp.where(left, packed, turned), jnp.where(left, turned, packed)], axis=0
        ).astype(jnp.bfloat16)
        term = lax.dot_general(
            picks[slot], block, (((0,), (0,)), ((), ())), preferred_element_type=jnp.float32
        )
        term = term * sides_ref[pl.ds(slot, 1), :]
        target_ref[slot] = term
        return mass + term, cross + term * seen_ref[slot].astype(jnp.float32)

    zero = jnp.zeros((tokens, LANES), jnp.float32)
    mass, cross = lax.fori_loop(0, MAXB, target_body, (zero, zero), unroll=2)
    sub_iota = lax.broadcasted_iota(jnp.int32, (8, LANES), 0)
    flip = lambda part: jnp.transpose(part)[:8]
    mine = jnp.where(sub_iota == 0, flip(top_at[...]), 0.0)
    mine = jnp.where(sub_iota == 1, flip(total_at[...]), mine)
    mine = jnp.where(sub_iota == 2, flip(picked_ref[...]), mine)
    mine = jnp.where(sub_iota == 3, flip(spread(jnp.sum(mass, axis=1, keepdims=True))), mine)
    mine = jnp.where(sub_iota == 4, flip(spread(jnp.sum(cross, axis=1, keepdims=True))), mine)
    own_sums[...] = mine
    sums[me] = mine
    for step, other in enumerate(others):
        copy = remote(own_sums, sums.at[me], send_sem.at[2, step], recv_sem.at[2, me], other)
        copy.start()
        copies.append(copy)
    for step, other in enumerate(others):
        remote(own_sums, sums.at[other], send_sem.at[2, step], recv_sem.at[2, other], other).wait_recv()
    parts = [sums[index] for index in range(count)]
    top = functools.reduce(jnp.maximum, [part[0:1] for part in parts])
    total = sum(part[1:2] * jnp.exp(part[0:1] - top) for part in parts)
    added = sum(parts)
    log_norm = top + jnp.log(total)
    weight = added[3:4] + 1.0
    loss = weight * log_norm - added[4:5] - added[2:3]
    loss_ref[...] = jnp.broadcast_to(loss, (8, LANES))
    shift_ref[...] = jnp.transpose(jnp.broadcast_to(log_norm - jnp.log(weight), (tokens, LANES)))
    for copy in copies:
        copy.wait_send()


def grad_kernel(tile_ref, first_ref, place_ref, ids_ref, shift_ref, target_ref, logits_ref, grad_ref, merged):
    width = logits_ref.shape[1]
    step = pl.program_id(0)
    shift = shift_ref[...]
    ids = ids_ref[...]

    @pl.when(step == 0)
    def _():
        merged[...] = jnp.zeros_like(merged)

        def body(slot, _):
            first = first_ref[slot]
            merged[first] = merged[first] + target_ref[slot]
            return _

        lax.fori_loop(0, MAXB, body, 0)

    def store(starts, parts):
        for start, part in zip(starts, parts):
            grad_ref[:, pl.ds(start, LANES)] = part.astype(jnp.bfloat16)

    def plain(start):
        return jnp.exp(logits_ref[:, pl.ds(start, LANES)].astype(jnp.float32) - shift)

    def body(index, _):
        starts = [pl.multiple_of(index * CHUNK + k, LANES) for k in range(0, CHUNK, LANES)]
        store(starts, [plain(start).astype(jnp.bfloat16) for start in starts])
        return _

    whole = width // CHUNK
    lax.fori_loop(0, whole, body, 0)
    starts = list(range(whole * CHUNK, width, LANES))
    store(starts, [plain(start) for start in starts])

    lane_iota = lax.broadcasted_iota(jnp.int32, (ROWS, LANES), 1)

    def marked(start):
        return plain(start) - jnp.where(lane_iota + start == ids, 1.0, 0.0)

    tiles = [place_ref[step * ROWS + row] for row in range(ROWS)]
    starts = [pl.multiple_of(tile * LANES, LANES) for tile in tiles]
    store(starts, [marked(start).astype(jnp.bfloat16) for start in starts])
    here = pl.ds(pl.multiple_of(step * ROWS, ROWS), ROWS)
    for begin in range(0, MAXB, 16):
        slots = range(begin, begin + 16)
        starts = [pl.multiple_of(tile_ref[slot] * LANES, LANES) for slot in slots]
        parts = [
            (marked(start) - merged[first_ref[slot], here, :]).astype(jnp.bfloat16)
            for slot, start in zip(slots, starts)
        ]
        store(starts, parts)


def params():
    return pltpu.CompilerParams(vmem_limit_bytes=LIMIT)


def local(
    teacher_logits, student_logits, token_ids, align_values, block_rows, block_cols, block_counts
):
    count = lax.axis_size("vocab")
    me = lax.axis_index("vocab")
    rows = teacher_logits.shape[0]
    width = student_logits.shape[1]
    padded = pl.cdiv(width, LANES) * LANES
    per_dest = MAXB // count
    steps = rows // ROWS
    smem = pl.BlockSpec(memory_space=SMEM)
    vmem = pl.BlockSpec(memory_space=VMEM)
    f32 = lambda *shape: jax.ShapeDtypeStruct(shape, jnp.float32)
    b16 = lambda *shape: jax.ShapeDtypeStruct(shape, jnp.bfloat16)

    live = lax.iota(jnp.int32, MAXB) < block_counts[0]
    sent_blocks = jnp.where(live[:, None], align_values, jnp.zeros_like(align_values))
    sent_blocks = sent_blocks.reshape(MAXB, 2, BLK // 2, BLK).transpose(0, 2, 1, 3)
    sent_blocks = sent_blocks.reshape(MAXB, BLK // 2, LANES)
    own_cols = jnp.broadcast_to(jnp.pad(block_cols, (0, LANES - MAXB))[None, :], (8, LANES))
    ids = token_ids - me * width
    size = rows * width
    dma = pltpu.SemaphoreType.DMA

    def comm_params(number):
        return pltpu.CompilerParams(
            vmem_limit_bytes=LIMIT, collective_id=number, has_side_effects=True
        )

    any_spec = pl.BlockSpec(memory_space=pl.ANY)
    stats, all_cols = pl.pallas_call(
        functools.partial(teacher_kernel, count),
        out_shape=(f32(8, LANES), jax.ShapeDtypeStruct((count, 8, LANES), jnp.int32)),
        in_specs=[vmem, vmem],
        out_specs=(vmem, vmem),
        scratch_shapes=[
            VMEM((rows, LANES), jnp.float32),
            VMEM((rows, LANES), jnp.float32),
            VMEM((8, LANES), jnp.float32),
            VMEM((count, 8, LANES), jnp.float32),
            VMEM((count, 8, LANES), jnp.int32),
            dma((2, count)),
            dma((2, count)),
        ],
        compiler_params=comm_params(1),
    )(own_cols, teacher_logits)

    cols = all_cols[:, 0, :MAXB].reshape(count, count, per_dest)
    cols = lax.dynamic_index_in_dim(cols, me, 1, keepdims=False).reshape(MAXB)
    tile = cols // 2
    first = jnp.argmax(tile[:, None] == tile[None, :], axis=1).astype(jnp.int32)
    place = jnp.clip(ids, 0, width - 1) // LANES
    sides = (lax.iota(jnp.int32, LANES)[None, :] // BLK == (cols % 2)[:, None]).astype(jnp.float32)

    whole_tiles = student_logits
    if padded != width:
        whole_tiles = jnp.pad(student_logits, ((0, 0), (0, padded - width)))
    picks, seen, picked = pl.pallas_call(
        pick_kernel,
        out_shape=(b16(MAXB, BLK, rows), b16(MAXB, rows, LANES), f32(rows, LANES)),
        in_specs=[smem, smem, smem, smem, vmem, vmem, any_spec],
        out_specs=(vmem, vmem, vmem),
        scratch_shapes=[VMEM((rows, ROWS, LANES), jnp.bfloat16), dma((MAXB,)), dma((rows,))],
        compiler_params=params(),
    )(block_rows, tile, ids, place, teacher_logits, stats, whole_tiles)

    target, shift, loss = pl.pallas_call(
        functools.partial(loss_kernel, count),
        out_shape=(f32(MAXB, rows, LANES), f32(rows, LANES), f32(8, LANES)),
        in_specs=[vmem, vmem, vmem, vmem, vmem, any_spec],
        out_specs=(vmem, vmem, vmem),
        scratch_shapes=[
            VMEM((rows, width), jnp.bfloat16),
            VMEM((rows, LANES), jnp.float32),
            VMEM((rows, LANES), jnp.float32),
            VMEM((8, LANES), jnp.float32),
            VMEM((count, 8, LANES), jnp.float32),
            VMEM((MAXB, BLK, rows), jnp.bfloat16),
            VMEM((MAXB, BLK // 2, LANES), jnp.bfloat16),
            dma((steps,)),
            dma((3, count)),
            dma((3, count)),
        ],
        compiler_params=comm_params(0),
    )(sides, picks, sent_blocks, seen, picked, student_logits)
    token_loss = loss[0]

    row_spec = pl.BlockSpec((ROWS, 1), lambda i: (i, 0))
    lane_spec = pl.BlockSpec((ROWS, LANES), lambda i: (i, 0))
    wide_spec = pl.BlockSpec((ROWS, padded), lambda i: (i, 0))
    logit_grad = pl.pallas_call(
        grad_kernel,
        out_shape=b16(rows, width),
        grid=(steps,),
        in_specs=[smem, smem, smem, row_spec, lane_spec, vmem, wide_spec],
        out_specs=wide_spec,
        scratch_shapes=[VMEM((MAXB, rows, LANES), jnp.float32)],
        compiler_params=params(),
        cost_estimate=pl.CostEstimate(flops=8 * size, bytes_accessed=4 * size, transcendentals=size),
    )(tile, first, place, ids[:, None], shift, target, student_logits)
    return logit_grad, token_loss


def solution(mesh):
    return jax.shard_map(
        local,
        mesh=mesh,
        in_specs=(
            P(("groups", "tok", "sub"), "vocab"),
            P(("groups", "tok", "sub"), "vocab"),
            P(("groups", "tok", "sub")),
            P("vocab", None),
            P("vocab"),
            P("vocab"),
            P("vocab"),
        ),
        out_specs=(P(("groups", "tok", "sub"), "vocab"), P(("groups", "tok", "sub"))),
        check_vma=False,
    )
```

```python
import functools

import jax
import jax.numpy as jnp
from jax import lax
from jax.experimental import pallas as pl
from jax.experimental.pallas import tpu as pltpu
from jax.sharding import PartitionSpec as P

BLK = 64
MAXB = 32
LANES = 128
ROWS = 16
CHUNK = 12800
VMEM = pltpu.VMEM
SMEM = pltpu.SMEM
LIMIT = 40 * 1024 * 1024


def lane_tile(index):
    return pl.ds(pl.multiple_of(index * LANES, LANES), LANES)


def fold(value, join):
    parts = [value[:, k : k + LANES] for k in range(0, value.shape[1], LANES)]
    ways = parts[:4]
    for index, part in enumerate(parts[4:]):
        ways[index % 4] = join(ways[index % 4], part)
    return functools.reduce(join, ways)


def row_stats(load, width):
    step = min(CHUNK, width // LANES * LANES)
    whole, tail = divmod(width, step)

    def chunk(index):
        return load(pl.multiple_of(index * step, LANES), step)

    def max_body(index, top):
        return jnp.maximum(top, fold(chunk(index), jnp.maximum))

    top = jnp.full((ROWS, LANES), -jnp.inf, jnp.bfloat16)
    top = lax.fori_loop(0, whole, max_body, top).astype(jnp.float32)
    top = jnp.max(top, axis=1, keepdims=True)
    if tail:
        rest = load(whole * step, tail).astype(jnp.float32)
        top = jnp.maximum(top, jnp.max(rest, axis=1, keepdims=True))

    def sum_body(index, total):
        return total + fold(jnp.exp(chunk(index).astype(jnp.float32) - top), jnp.add)

    total = lax.fori_loop(0, whole, sum_body, jnp.zeros((ROWS, LANES), jnp.float32))
    total = jnp.sum(total, axis=1, keepdims=True)
    if tail:
        total = total + jnp.sum(jnp.exp(rest - top), axis=1, keepdims=True)
    return top, total


def greet(others):
    barrier = pltpu.get_barrier_semaphore()
    for other in others:
        pl.semaphore_signal(
            barrier, inc=1, device_id={"vocab": other}, device_id_type=pl.DeviceIdType.MESH
        )
    return barrier


def remote(source, target, send_sem, recv_sem, other):
    return pltpu.make_async_remote_copy(
        src_ref=source,
        dst_ref=target,
        send_sem=send_sem,
        recv_sem=recv_sem,
        device_id={"vocab": other},
        device_id_type=pl.DeviceIdType.MESH,
    )


def rows_of(index):
    return pl.ds(pl.multiple_of(index * ROWS, ROWS), ROWS)


def spread(part):
    return jnp.broadcast_to(part, (part.shape[0], LANES))


def teacher_kernel(
    count, cols_ref, teacher_ref, stats_ref, all_cols_ref,
    logits, top_at, total_at, own_stats, stats, own_cols, cols, load_sem, send_sem, recv_sem,
):
    me = lax.axis_index("vocab")
    others = [lax.rem(me + step, count) for step in range(1, count)]

    def load(index):
        return pltpu.make_async_copy(
            teacher_ref.at[rows_of(index)], logits.at[rows_of(index)], load_sem.at[index]
        )

    for index in range(logits.shape[0] // ROWS):
        load(index).start()
    barrier = greet(others)
    spare = jnp.zeros((1, LANES - MAXB), jnp.int32)
    own_cols[...] = jnp.broadcast_to(jnp.concatenate([cols_ref[...], spare], axis=1), (8, LANES))

    def body(index, _):
        load(index).wait()
        here = rows_of(index)
        top, total = row_stats(lambda start, size: logits[here, pl.ds(start, size)], logits.shape[1])
        top_at[here, :] = spread(top)
        total_at[here, :] = spread(total)
        return _

    lax.fori_loop(0, logits.shape[0] // ROWS, body, 0)
    sub_iota = lax.broadcasted_iota(jnp.int32, (8, LANES), 0)
    own_stats[...] = jnp.where(
        sub_iota == 0, jnp.transpose(top_at[...])[:8], jnp.transpose(total_at[...])[:8]
    )
    stats[me] = own_stats[...]
    cols[me] = own_cols[...]
    pl.semaphore_wait(barrier, count - 1)
    copies = []
    for step, other in enumerate(others):
        copies.append(remote(own_stats, stats.at[me], send_sem.at[0, step], recv_sem.at[0, me], other))
        copies.append(remote(own_cols, cols.at[me], send_sem.at[1, step], recv_sem.at[1, me], other))
    for copy in copies:
        copy.start()
    for step, other in enumerate(others):
        remote(own_stats, stats.at[other], send_sem.at[0, step], recv_sem.at[0, other], other).wait_recv()
        remote(own_cols, cols.at[other], send_sem.at[1, step], recv_sem.at[1, other], other).wait_recv()
    tops = [stats[index, 0:1] for index in range(count)]
    totals = [stats[index, 1:2] for index in range(count)]
    top = functools.reduce(jnp.maximum, tops)
    total = sum(part * jnp.exp(peak - top) for part, peak in zip(totals, tops))
    stats_ref[...] = jnp.where(sub_iota == 0, top, total)
    all_cols_ref[...] = cols[...]
    for copy in copies:
        copy.wait_send()


def pick_kernel(
    rows_ref, count_ref, tile_ref, ids_ref, place_ref, align_ref, teacher_ref, stats_ref, student_ref,
    picks_ref, blocks_ref, seen_ref, picked_ref,
    teacher, near, turned, packed, teacher_sem, seen_sem, near_sem,
):
    tokens = teacher_ref.shape[0]
    teacher_copy = pltpu.make_async_copy(teacher_ref, teacher, teacher_sem)
    teacher_copy.start()

    def near_copy(token):
        return pltpu.make_async_copy(
            student_ref.at[rows_of(token // ROWS), lane_tile(place_ref[token])],
            near.at[token],
            near_sem.at[token],
        )

    def seen_copy(slot):
        return pltpu.make_async_copy(
            student_ref.at[:, lane_tile(tile_ref[slot])], seen_ref.at[slot], seen_sem.at[slot]
        )

    def start_near(token, _):
        near_copy(token).start()
        return _

    def start_seen(slot, _):
        seen_copy(slot).start()
        return _

    lax.fori_loop(0, tokens, start_near, 0, unroll=8)
    lax.fori_loop(0, MAXB, start_seen, 0, unroll=8)
    live = lax.broadcasted_iota(jnp.int32, (MAXB, LANES), 0) < count_ref[0]
    lines = BLK * BLK // LANES
    for line in range(lines):
        part = align_ref[:, line * LANES : (line + 1) * LANES].astype(jnp.float32)
        packed[pl.ds(line, MAXB, stride=lines), :] = jnp.where(live, part, 0.0)
    for slot in range(MAXB):
        blocks_ref[slot] = packed[slot * lines : (slot + 1) * lines, :].astype(jnp.bfloat16)
    top = stats_ref[0:1]
    total = stats_ref[1:2]
    teacher_copy.wait()

    def body(slot, _):
        row = rows_ref[slot]
        scores = jnp.transpose(teacher[:, lane_tile(row // 2)].astype(jnp.float32))
        scores = jnp.where(row % 2 == 0, scores[:BLK], scores[BLK:])
        turned[slot] = jnp.exp(scores - top) / total
        even = turned[slot, pl.ds(0, BLK // 2, stride=2), :]
        odd = turned[slot, pl.ds(1, BLK // 2, stride=2), :]
        picks_ref[slot] = jnp.concatenate([even, odd], axis=0).astype(jnp.bfloat16)
        return _

    lax.fori_loop(0, MAXB, body, 0, unroll=4)

    row_iota = lax.broadcasted_iota(jnp.int32, (ROWS, LANES), 0)
    lane_iota = lax.broadcasted_iota(jnp.int32, (ROWS, LANES), 1)

    def picked_body(index, _):
        picked = jnp.zeros((ROWS, LANES), jnp.float32)
        for row in range(ROWS):
            token = index * ROWS + row
            near_copy(token).wait()
            hit = (row_iota == row) & (lane_iota == ids_ref[token] - place_ref[token] * LANES)
            picked = jnp.where(hit, near[token].astype(jnp.float32), picked)
        picked_ref[rows_of(index), :] = spread(jnp.sum(picked, axis=1, keepdims=True))
        return _

    lax.fori_loop(0, tokens // ROWS, picked_body, 0)

    def wait_seen(slot, _):
        seen_copy(slot).wait()
        return _

    lax.fori_loop(0, MAXB, wait_seen, 0, unroll=8)


def loss_kernel(
    count, sides_ref, picks_ref, blocks_ref, seen_ref, picked_ref, student_ref,
    target_ref, shift_ref, loss_ref,
    logits, top_at, total_at, own_sums, sums, picks, blocks, load_sem, send_sem, recv_sem,
):
    me = lax.axis_index("vocab")
    tokens, width = logits.shape
    per = MAXB // count
    others = [lax.rem(me + step, count) for step in range(1, count)]
    slots = lambda owner: pl.ds(owner * per, per)

    def load(index):
        return pltpu.make_async_copy(
            student_ref.at[rows_of(index)], logits.at[rows_of(index)], load_sem.at[index]
        )

    for index in range(tokens // ROWS):
        load(index).start()
    barrier = greet(others)
    for slot in range(per):
        blocks[me * per + slot] = blocks_ref[me * per + slot]
        picks[me * per + slot] = picks_ref[me * per + slot]
    pl.semaphore_wait(barrier, count - 1)
    copies = []
    for step, other in enumerate(others):
        for kind, source, buffer in ((0, picks_ref, picks), (1, blocks_ref, blocks)):
            copies.append(
                remote(
                    source.at[slots(other)], buffer.at[slots(me)],
                    send_sem.at[kind, step], recv_sem.at[kind, me], other,
                )
            )
    for copy in copies:
        copy.start()

    def student_body(index, _):
        load(index).wait()
        here = rows_of(index)
        top, total = row_stats(lambda start, size: logits[here, pl.ds(start, size)], width)
        top_at[here, :] = spread(top)
        total_at[here, :] = spread(total)
        return _

    lax.fori_loop(0, tokens // ROWS, student_body, 0)

    for step, other in enumerate(others):
        for kind, source, buffer in ((0, picks_ref, picks), (1, blocks_ref, blocks)):
            remote(
                source.at[slots(other)], buffer.at[slots(other)],
                send_sem.at[kind, step], recv_sem.at[kind, other], other,
            ).wait_recv()

    left = lax.broadcasted_iota(jnp.int32, (1, LANES), 1) < BLK

    def target_body(slot, carry):
        mass, cross = carry
        packed = blocks[slot].astype(jnp.float32)
        turned = pltpu.roll(packed, BLK, 1)
        block = jnp.concatenate(
            [jnp.where(left, packed, turned), jnp.where(left, turned, packed)], axis=0
        ).astype(jnp.bfloat16)
        term = lax.dot_general(
            picks[slot], block, (((0,), (0,)), ((), ())), preferred_element_type=jnp.float32
        )
        term = term * sides_ref[pl.ds(slot, 1), :]
        target_ref[slot] = term
        return mass + term, cross + term * seen_ref[slot].astype(jnp.float32)

    zero = jnp.zeros((tokens, LANES), jnp.float32)
    mass, cross = lax.fori_loop(0, MAXB, target_body, (zero, zero), unroll=4)
    sub_iota = lax.broadcasted_iota(jnp.int32, (8, LANES), 0)
    flip = lambda part: jnp.transpose(part)[:8]
    mine = jnp.where(sub_iota == 0, flip(top_at[...]), 0.0)
    mine = jnp.where(sub_iota == 1, flip(total_at[...]), mine)
    mine = jnp.where(sub_iota == 2, flip(picked_ref[...]), mine)
    mine = jnp.where(sub_iota == 3, flip(spread(jnp.sum(mass, axis=1, keepdims=True))), mine)
    mine = jnp.where(sub_iota == 4, flip(spread(jnp.sum(cross, axis=1, keepdims=True))), mine)
    own_sums[...] = mine
    sums[me] = mine
    for step, other in enumerate(others):
        copy = remote(own_sums, sums.at[me], send_sem.at[2, step], recv_sem.at[2, me], other)
        copy.start()
        copies.append(copy)
    for step, other in enumerate(others):
        remote(own_sums, sums.at[other], send_sem.at[2, step], recv_sem.at[2, other], other).wait_recv()
    parts = [sums[index] for index in range(count)]
    top = functools.reduce(jnp.maximum, [part[0:1] for part in parts])
    total = sum(part[1:2] * jnp.exp(part[0:1] - top) for part in parts)
    added = sum(parts)
    log_norm = top + jnp.log(total)
    weight = added[3:4] + 1.0
    loss = weight * log_norm - added[4:5] - added[2:3]
    loss_ref[...] = loss
    shift_ref[...] = jnp.transpose(jnp.broadcast_to(log_norm - jnp.log(weight), (tokens, LANES)))
    for copy in copies:
        copy.wait_send()


def grad_kernel(tile_ref, first_ref, place_ref, ids_ref, shift_ref, target_ref, logits_ref, grad_ref, merged):
    width = logits_ref.shape[1]
    step = pl.program_id(0)
    shift = shift_ref[...]
    ids = ids_ref[...]

    @pl.when(step == 0)
    def _():
        merged[...] = jnp.zeros_like(merged)

        def body(slot, _):
            first = first_ref[slot]
            merged[first] = merged[first] + target_ref[slot]
            return _

        lax.fori_loop(0, MAXB, body, 0)

    def store(starts, parts):
        for start, part in zip(starts, parts):
            grad_ref[:, pl.ds(start, LANES)] = part.astype(jnp.bfloat16)

    def plain(start):
        return jnp.exp(logits_ref[:, pl.ds(start, LANES)].astype(jnp.float32) - shift)

    def body(index, _):
        starts = [pl.multiple_of(index * CHUNK + k, LANES) for k in range(0, CHUNK, LANES)]
        store(starts, [plain(start).astype(jnp.bfloat16) for start in starts])
        return _

    whole = width // CHUNK
    lax.fori_loop(0, whole, body, 0)
    starts = list(range(whole * CHUNK, width, LANES))
    store(starts, [plain(start) for start in starts])

    lane_iota = lax.broadcasted_iota(jnp.int32, (ROWS, LANES), 1)

    def marked(start):
        return plain(start) - jnp.where(lane_iota + start == ids, 1.0, 0.0)

    tiles = [place_ref[step * ROWS + row] for row in range(ROWS)]
    starts = [pl.multiple_of(tile * LANES, LANES) for tile in tiles]
    store(starts, [marked(start).astype(jnp.bfloat16) for start in starts])
    here = pl.ds(pl.multiple_of(step * ROWS, ROWS), ROWS)
    for begin in range(0, MAXB, 16):
        slots = range(begin, begin + 16)
        starts = [pl.multiple_of(tile_ref[slot] * LANES, LANES) for slot in slots]
        parts = [
            (marked(start) - merged[first_ref[slot], here, :]).astype(jnp.bfloat16)
            for slot, start in zip(slots, starts)
        ]
        store(starts, parts)


def params():
    return pltpu.CompilerParams(vmem_limit_bytes=LIMIT)


def local(
    teacher_logits, student_logits, token_ids, align_values, block_rows, block_cols, block_counts
):
    count = lax.axis_size("vocab")
    me = lax.axis_index("vocab")
    rows = teacher_logits.shape[0]
    width = student_logits.shape[1]
    padded = pl.cdiv(width, LANES) * LANES
    per_dest = MAXB // count
    steps = rows // ROWS
    smem = pl.BlockSpec(memory_space=SMEM)
    vmem = pl.BlockSpec(memory_space=VMEM)
    f32 = lambda *shape: jax.ShapeDtypeStruct(shape, jnp.float32)
    b16 = lambda *shape: jax.ShapeDtypeStruct(shape, jnp.bfloat16)

    ids = token_ids - me * width
    size = rows * width
    dma = pltpu.SemaphoreType.DMA

    def comm_params(number):
        return pltpu.CompilerParams(
            vmem_limit_bytes=LIMIT, collective_id=number, has_side_effects=True
        )

    any_spec = pl.BlockSpec(memory_space=pl.ANY)
    stats, all_cols = pl.pallas_call(
        functools.partial(teacher_kernel, count),
        out_shape=(f32(8, LANES), jax.ShapeDtypeStruct((count, 8, LANES), jnp.int32)),
        in_specs=[vmem, any_spec],
        out_specs=(vmem, vmem),
        scratch_shapes=[
            VMEM(teacher_logits.shape, jnp.bfloat16),
            VMEM((rows, LANES), jnp.float32),
            VMEM((rows, LANES), jnp.float32),
            VMEM((8, LANES), jnp.float32),
            VMEM((count, 8, LANES), jnp.float32),
            VMEM((8, LANES), jnp.int32),
            VMEM((count, 8, LANES), jnp.int32),
            dma((steps,)),
            dma((2, count)),
            dma((2, count)),
        ],
        compiler_params=comm_params(1),
    )(block_cols[None, :], teacher_logits)

    cols = all_cols[:, 0, :MAXB].reshape(count, count, per_dest)
    cols = lax.dynamic_index_in_dim(cols, me, 1, keepdims=False).reshape(MAXB)
    tile = cols // 2
    first = jnp.argmax(tile[:, None] == tile[None, :], axis=1).astype(jnp.int32)
    place = jnp.clip(ids, 0, width - 1) // LANES
    sides = (lax.iota(jnp.int32, LANES)[None, :] // BLK == (cols % 2)[:, None]).astype(jnp.float32)

    whole_tiles = student_logits
    if padded != width:
        whole_tiles = jnp.pad(student_logits, ((0, 0), (0, padded - width)))
    picks, sent_blocks, seen, picked = pl.pallas_call(
        pick_kernel,
        out_shape=(
            b16(MAXB, BLK, rows),
            b16(MAXB, BLK // 2, LANES),
            b16(MAXB, rows, LANES),
            f32(rows, LANES),
        ),
        in_specs=[smem, smem, smem, smem, smem, vmem, any_spec, vmem, any_spec],
        out_specs=(vmem, vmem, vmem, vmem),
        scratch_shapes=[
            VMEM(teacher_logits.shape, jnp.bfloat16),
            VMEM((rows, ROWS, LANES), jnp.bfloat16),
            VMEM((MAXB, BLK, rows), jnp.float32),
            VMEM((MAXB * BLK // 2, LANES), jnp.float32),
            dma,
            dma((MAXB,)),
            dma((rows,)),
        ],
        compiler_params=params(),
    )(block_rows, block_counts, tile, ids, place, align_values, teacher_logits, stats, whole_tiles)

    target, shift, loss = pl.pallas_call(
        functools.partial(loss_kernel, count),
        out_shape=(f32(MAXB, rows, LANES), f32(rows, LANES), f32(1, LANES)),
        in_specs=[vmem, vmem, vmem, vmem, vmem, any_spec],
        out_specs=(vmem, vmem, vmem),
        scratch_shapes=[
            VMEM((rows, width), jnp.bfloat16),
            VMEM((rows, LANES), jnp.float32),
            VMEM((rows, LANES), jnp.float32),
            VMEM((8, LANES), jnp.float32),
            VMEM((count, 8, LANES), jnp.float32),
            VMEM((MAXB, BLK, rows), jnp.bfloat16),
            VMEM((MAXB, BLK // 2, LANES), jnp.bfloat16),
            dma((steps,)),
            dma((3, count)),
            dma((3, count)),
        ],
        compiler_params=comm_params(0),
    )(sides, picks, sent_blocks, seen, picked, student_logits)
    token_loss = loss.reshape(rows)

    row_spec = pl.BlockSpec((ROWS, 1), lambda i: (i, 0))
    lane_spec = pl.BlockSpec((ROWS, LANES), lambda i: (i, 0))
    wide_spec = pl.BlockSpec((ROWS, padded), lambda i: (i, 0))
    logit_grad = pl.pallas_call(
        grad_kernel,
        out_shape=b16(rows, width),
        grid=(steps,),
        in_specs=[smem, smem, smem, row_spec, lane_spec, vmem, wide_spec],
        out_specs=wide_spec,
        scratch_shapes=[VMEM((MAXB, rows, LANES), jnp.float32)],
        compiler_params=params(),
        cost_estimate=pl.CostEstimate(flops=8 * size, bytes_accessed=4 * size, transcendentals=size),
    )(tile, first, place, ids[:, None], shift, target, student_logits)
    return logit_grad, token_loss


def solution(mesh):
    return jax.shard_map(
        local,
        mesh=mesh,
        in_specs=(
            P(("groups", "tok", "sub"), "vocab"),
            P(("groups", "tok", "sub"), "vocab"),
            P(("groups", "tok", "sub")),
            P("vocab", None),
            P("vocab"),
            P("vocab"),
            P("vocab"),
        ),
        out_specs=(P(("groups", "tok", "sub"), "vocab"), P(("groups", "tok", "sub"))),
        check_vma=False,
    )
```

```python
import functools

import jax
import jax.numpy as jnp
from jax import lax
from jax.experimental import pallas as pl
from jax.experimental.pallas import tpu as pltpu
from jax.sharding import PartitionSpec as P

BLK = 64
MAXB = 32
LANES = 128
ROWS = 16
EARLY = 3
CHUNK = 12800
VMEM = pltpu.VMEM
SMEM = pltpu.SMEM
LIMIT = 40 * 1024 * 1024


def lane_tile(index):
    return pl.ds(pl.multiple_of(index * LANES, LANES), LANES)


def fold(value, join):
    parts = [value[:, k : k + LANES] for k in range(0, value.shape[1], LANES)]
    ways = parts[:4]
    for index, part in enumerate(parts[4:]):
        ways[index % 4] = join(ways[index % 4], part)
    return functools.reduce(join, ways)


def row_stats(load, width):
    step = min(CHUNK, width // LANES * LANES)
    whole, tail = divmod(width, step)

    def chunk(index):
        return load(pl.multiple_of(index * step, LANES), step)

    def max_body(index, top):
        return jnp.maximum(top, fold(chunk(index), jnp.maximum))

    top = jnp.full((ROWS, LANES), -jnp.inf, jnp.bfloat16)
    top = lax.fori_loop(0, whole, max_body, top).astype(jnp.float32)
    top = jnp.max(top, axis=1, keepdims=True)
    if tail:
        rest = load(whole * step, tail).astype(jnp.float32)
        top = jnp.maximum(top, jnp.max(rest, axis=1, keepdims=True))

    def sum_body(index, total):
        return total + fold(jnp.exp(chunk(index).astype(jnp.float32) - top), jnp.add)

    total = lax.fori_loop(0, whole, sum_body, jnp.zeros((ROWS, LANES), jnp.float32))
    total = jnp.sum(total, axis=1, keepdims=True)
    if tail:
        total = total + jnp.sum(jnp.exp(rest - top), axis=1, keepdims=True)
    return top, total


def greet(others):
    barrier = pltpu.get_barrier_semaphore()
    for other in others:
        pl.semaphore_signal(
            barrier, inc=1, device_id={"vocab": other}, device_id_type=pl.DeviceIdType.MESH
        )
    return barrier


def remote(source, target, send_sem, recv_sem, other):
    return pltpu.make_async_remote_copy(
        src_ref=source,
        dst_ref=target,
        send_sem=send_sem,
        recv_sem=recv_sem,
        device_id={"vocab": other},
        device_id_type=pl.DeviceIdType.MESH,
    )


def rows_of(index):
    return pl.ds(pl.multiple_of(index * ROWS, ROWS), ROWS)


def spread(part):
    return jnp.broadcast_to(part, (part.shape[0], LANES))


def teacher_kernel(
    count, cols_ref, teacher_ref, student_ref, stats_ref, all_cols_ref, early_top_ref, early_total_ref,
    logits, student, student_sem, top_at, total_at, own_stats, stats, own_cols, cols, load_sem, send_sem, recv_sem,
):
    me = lax.axis_index("vocab")
    others = [lax.rem(me + step, count) for step in range(1, count)]

    def load(index):
        return pltpu.make_async_copy(
            teacher_ref.at[rows_of(index)], logits.at[rows_of(index)], load_sem.at[index]
        )

    def load_student(index):
        return pltpu.make_async_copy(
            student_ref.at[rows_of(index)], student.at[rows_of(index)], student_sem.at[index]
        )

    for index in range(logits.shape[0] // ROWS):
        load(index).start()
    for index in range(EARLY):
        load_student(index).start()
    barrier = greet(others)
    spare = jnp.zeros((1, LANES - MAXB), jnp.int32)
    own_cols[...] = jnp.broadcast_to(jnp.concatenate([cols_ref[...], spare], axis=1), (8, LANES))

    def body(index, _):
        load(index).wait()
        here = rows_of(index)
        top, total = row_stats(lambda start, size: logits[here, pl.ds(start, size)], logits.shape[1])
        top_at[here, :] = spread(top)
        total_at[here, :] = spread(total)
        return _

    lax.fori_loop(0, logits.shape[0] // ROWS, body, 0)
    sub_iota = lax.broadcasted_iota(jnp.int32, (8, LANES), 0)
    own_stats[...] = jnp.where(
        sub_iota == 0, jnp.transpose(top_at[...])[:8], jnp.transpose(total_at[...])[:8]
    )
    stats[me] = own_stats[...]
    cols[me] = own_cols[...]
    pl.semaphore_wait(barrier, count - 1)
    copies = []
    for step, other in enumerate(others):
        copies.append(remote(own_stats, stats.at[me], send_sem.at[0, step], recv_sem.at[0, me], other))
        copies.append(remote(own_cols, cols.at[me], send_sem.at[1, step], recv_sem.at[1, me], other))
    for copy in copies:
        copy.start()

    def student_body(index, _):
        load_student(index).wait()
        here = rows_of(index)
        top, total = row_stats(lambda start, size: student[here, pl.ds(start, size)], student.shape[1])
        early_top_ref[here, :] = spread(top)
        early_total_ref[here, :] = spread(total)
        return _

    lax.fori_loop(0, EARLY, student_body, 0)
    for step, other in enumerate(others):
        remote(own_stats, stats.at[other], send_sem.at[0, step], recv_sem.at[0, other], other).wait_recv()
        remote(own_cols, cols.at[other], send_sem.at[1, step], recv_sem.at[1, other], other).wait_recv()
    tops = [stats[index, 0:1] for index in range(count)]
    totals = [stats[index, 1:2] for index in range(count)]
    top = functools.reduce(jnp.maximum, tops)
    total = sum(part * jnp.exp(peak - top) for part, peak in zip(totals, tops))
    stats_ref[...] = jnp.where(sub_iota == 0, top, total)
    all_cols_ref[...] = cols[...]
    for copy in copies:
        copy.wait_send()


def pick_kernel(
    rows_ref, count_ref, tile_ref, ids_ref, place_ref, align_ref, teacher_ref, stats_ref, student_ref,
    picks_ref, blocks_ref, seen_ref, picked_ref,
    teacher, near, turned, packed, teacher_sem, seen_sem, near_sem,
):
    tokens = teacher_ref.shape[0]
    teacher_copy = pltpu.make_async_copy(teacher_ref, teacher, teacher_sem)
    teacher_copy.start()

    def near_copy(token):
        return pltpu.make_async_copy(
            student_ref.at[rows_of(token // ROWS), lane_tile(place_ref[token])],
            near.at[token],
            near_sem.at[token],
        )

    def seen_copy(slot):
        return pltpu.make_async_copy(
            student_ref.at[:, lane_tile(tile_ref[slot])], seen_ref.at[slot], seen_sem.at[slot]
        )

    def start_near(token, _):
        near_copy(token).start()
        return _

    def start_seen(slot, _):
        seen_copy(slot).start()
        return _

    lax.fori_loop(0, tokens, start_near, 0, unroll=8)
    lax.fori_loop(0, MAXB, start_seen, 0, unroll=8)
    live = lax.broadcasted_iota(jnp.int32, (MAXB, LANES), 0) < count_ref[0]
    lines = BLK * BLK // LANES
    for line in range(lines):
        part = align_ref[:, line * LANES : (line + 1) * LANES].astype(jnp.float32)
        packed[pl.ds(line, MAXB, stride=lines), :] = jnp.where(live, part, 0.0)
    for slot in range(MAXB):
        blocks_ref[slot] = packed[slot * lines : (slot + 1) * lines, :].astype(jnp.bfloat16)
    top = stats_ref[0:1]
    total = stats_ref[1:2]
    teacher_copy.wait()

    def body(slot, _):
        row = rows_ref[slot]
        scores = jnp.transpose(teacher[:, lane_tile(row // 2)].astype(jnp.float32))
        scores = jnp.where(row % 2 == 0, scores[:BLK], scores[BLK:])
        turned[slot] = jnp.exp(scores - top) / total
        even = turned[slot, pl.ds(0, BLK // 2, stride=2), :]
        odd = turned[slot, pl.ds(1, BLK // 2, stride=2), :]
        picks_ref[slot] = jnp.concatenate([even, odd], axis=0).astype(jnp.bfloat16)
        return _

    lax.fori_loop(0, MAXB, body, 0, unroll=4)

    row_iota = lax.broadcasted_iota(jnp.int32, (ROWS, LANES), 0)
    lane_iota = lax.broadcasted_iota(jnp.int32, (ROWS, LANES), 1)

    def picked_body(index, _):
        picked = jnp.zeros((ROWS, LANES), jnp.float32)
        for row in range(ROWS):
            token = index * ROWS + row
            near_copy(token).wait()
            hit = (row_iota == row) & (lane_iota == ids_ref[token] - place_ref[token] * LANES)
            picked = jnp.where(hit, near[token].astype(jnp.float32), picked)
        picked_ref[rows_of(index), :] = spread(jnp.sum(picked, axis=1, keepdims=True))
        return _

    lax.fori_loop(0, tokens // ROWS, picked_body, 0)

    def wait_seen(slot, _):
        seen_copy(slot).wait()
        return _

    lax.fori_loop(0, MAXB, wait_seen, 0, unroll=8)


def loss_kernel(
    count, sides_ref, picks_ref, blocks_ref, seen_ref, picked_ref, early_top_ref, early_total_ref, student_ref,
    target_ref, shift_ref, loss_ref,
    logits, top_at, total_at, own_sums, sums, picks, blocks, load_sem, send_sem, recv_sem,
):
    me = lax.axis_index("vocab")
    tokens, width = logits.shape
    per = MAXB // count
    others = [lax.rem(me + step, count) for step in range(1, count)]
    slots = lambda owner: pl.ds(owner * per, per)

    def load(index):
        return pltpu.make_async_copy(
            student_ref.at[rows_of(index)], logits.at[rows_of(index)], load_sem.at[index]
        )

    for index in range(EARLY, tokens // ROWS):
        load(index).start()
    barrier = greet(others)
    top_at[: EARLY * ROWS, :] = early_top_ref[...]
    total_at[: EARLY * ROWS, :] = early_total_ref[...]
    for slot in range(per):
        blocks[me * per + slot] = blocks_ref[me * per + slot]
        picks[me * per + slot] = picks_ref[me * per + slot]
    pl.semaphore_wait(barrier, count - 1)
    copies = []
    for step, other in enumerate(others):
        for kind, source, buffer in ((0, picks_ref, picks), (1, blocks_ref, blocks)):
            copies.append(
                remote(
                    source.at[slots(other)], buffer.at[slots(me)],
                    send_sem.at[kind, step], recv_sem.at[kind, me], other,
                )
            )
    for copy in copies:
        copy.start()

    def student_body(index, _):
        load(index).wait()
        here = rows_of(index)
        top, total = row_stats(lambda start, size: logits[here, pl.ds(start, size)], width)
        top_at[here, :] = spread(top)
        total_at[here, :] = spread(total)
        return _

    lax.fori_loop(EARLY, tokens // ROWS, student_body, 0)

    for step, other in enumerate(others):
        for kind, source, buffer in ((0, picks_ref, picks), (1, blocks_ref, blocks)):
            remote(
                source.at[slots(other)], buffer.at[slots(other)],
                send_sem.at[kind, step], recv_sem.at[kind, other], other,
            ).wait_recv()

    left = lax.broadcasted_iota(jnp.int32, (1, LANES), 1) < BLK

    def target_body(slot, carry):
        mass, cross = carry
        packed = blocks[slot].astype(jnp.float32)
        turned = pltpu.roll(packed, BLK, 1)
        block = jnp.concatenate(
            [jnp.where(left, packed, turned), jnp.where(left, turned, packed)], axis=0
        ).astype(jnp.bfloat16)
        term = lax.dot_general(
            picks[slot], block, (((0,), (0,)), ((), ())), preferred_element_type=jnp.float32
        )
        term = term * sides_ref[pl.ds(slot, 1), :]
        target_ref[slot] = term
        return mass + term, cross + term * seen_ref[slot].astype(jnp.float32)

    zero = jnp.zeros((tokens, LANES), jnp.float32)
    mass, cross = lax.fori_loop(0, MAXB, target_body, (zero, zero), unroll=4)
    sub_iota = lax.broadcasted_iota(jnp.int32, (8, LANES), 0)
    flip = lambda part: jnp.transpose(part)[:8]
    mine = jnp.where(sub_iota == 0, flip(top_at[...]), 0.0)
    mine = jnp.where(sub_iota == 1, flip(total_at[...]), mine)
    mine = jnp.where(sub_iota == 2, flip(picked_ref[...]), mine)
    mine = jnp.where(sub_iota == 3, flip(spread(jnp.sum(mass, axis=1, keepdims=True))), mine)
    mine = jnp.where(sub_iota == 4, flip(spread(jnp.sum(cross, axis=1, keepdims=True))), mine)
    own_sums[...] = mine
    sums[me] = mine
    for step, other in enumerate(others):
        copy = remote(own_sums, sums.at[me], send_sem.at[2, step], recv_sem.at[2, me], other)
        copy.start()
        copies.append(copy)
    for step, other in enumerate(others):
        remote(own_sums, sums.at[other], send_sem.at[2, step], recv_sem.at[2, other], other).wait_recv()
    parts = [sums[index] for index in range(count)]
    top = functools.reduce(jnp.maximum, [part[0:1] for part in parts])
    total = sum(part[1:2] * jnp.exp(part[0:1] - top) for part in parts)
    added = sum(parts)
    log_norm = top + jnp.log(total)
    weight = added[3:4] + 1.0
    loss = weight * log_norm - added[4:5] - added[2:3]
    loss_ref[...] = loss
    shift_ref[...] = jnp.transpose(jnp.broadcast_to(log_norm - jnp.log(weight), (tokens, LANES)))
    for copy in copies:
        copy.wait_send()


def grad_kernel(tile_ref, first_ref, place_ref, ids_ref, shift_ref, target_ref, logits_ref, grad_ref, merged):
    width = logits_ref.shape[1]
    step = pl.program_id(0)
    shift = shift_ref[...]
    ids = ids_ref[...]

    @pl.when(step == 0)
    def _():
        merged[...] = jnp.zeros_like(merged)

        def body(slot, _):
            first = first_ref[slot]
            merged[first] = merged[first] + target_ref[slot]
            return _

        lax.fori_loop(0, MAXB, body, 0)

    def store(starts, parts):
        for start, part in zip(starts, parts):
            grad_ref[:, pl.ds(start, LANES)] = part.astype(jnp.bfloat16)

    def plain(start):
        return jnp.exp(logits_ref[:, pl.ds(start, LANES)].astype(jnp.float32) - shift)

    def body(index, _):
        starts = [pl.multiple_of(index * CHUNK + k, LANES) for k in range(0, CHUNK, LANES)]
        store(starts, [plain(start).astype(jnp.bfloat16) for start in starts])
        return _

    whole = width // CHUNK
    lax.fori_loop(0, whole, body, 0)
    starts = list(range(whole * CHUNK, width, LANES))
    store(starts, [plain(start) for start in starts])

    lane_iota = lax.broadcasted_iota(jnp.int32, (ROWS, LANES), 1)

    def marked(start):
        return plain(start) - jnp.where(lane_iota + start == ids, 1.0, 0.0)

    tiles = [place_ref[step * ROWS + row] for row in range(ROWS)]
    starts = [pl.multiple_of(tile * LANES, LANES) for tile in tiles]
    store(starts, [marked(start).astype(jnp.bfloat16) for start in starts])
    here = pl.ds(pl.multiple_of(step * ROWS, ROWS), ROWS)
    for begin in range(0, MAXB, 16):
        slots = range(begin, begin + 16)
        starts = [pl.multiple_of(tile_ref[slot] * LANES, LANES) for slot in slots]
        parts = [
            (marked(start) - merged[first_ref[slot], here, :]).astype(jnp.bfloat16)
            for slot, start in zip(slots, starts)
        ]
        store(starts, parts)


def params():
    return pltpu.CompilerParams(vmem_limit_bytes=LIMIT)


def local(
    teacher_logits, student_logits, token_ids, align_values, block_rows, block_cols, block_counts
):
    count = lax.axis_size("vocab")
    me = lax.axis_index("vocab")
    rows = teacher_logits.shape[0]
    width = student_logits.shape[1]
    padded = pl.cdiv(width, LANES) * LANES
    per_dest = MAXB // count
    steps = rows // ROWS
    smem = pl.BlockSpec(memory_space=SMEM)
    vmem = pl.BlockSpec(memory_space=VMEM)
    f32 = lambda *shape: jax.ShapeDtypeStruct(shape, jnp.float32)
    b16 = lambda *shape: jax.ShapeDtypeStruct(shape, jnp.bfloat16)

    ids = token_ids - me * width
    size = rows * width
    dma = pltpu.SemaphoreType.DMA

    def comm_params(number):
        return pltpu.CompilerParams(
            vmem_limit_bytes=LIMIT, collective_id=number, has_side_effects=True
        )

    any_spec = pl.BlockSpec(memory_space=pl.ANY)
    stats, all_cols, early_top, early_total = pl.pallas_call(
        functools.partial(teacher_kernel, count),
        out_shape=(
            f32(8, LANES),
            jax.ShapeDtypeStruct((count, 8, LANES), jnp.int32),
            f32(EARLY * ROWS, LANES),
            f32(EARLY * ROWS, LANES),
        ),
        in_specs=[vmem, any_spec, any_spec],
        out_specs=(vmem, vmem, vmem, vmem),
        scratch_shapes=[
            VMEM(teacher_logits.shape, jnp.bfloat16),
            VMEM((EARLY * ROWS, width), jnp.bfloat16),
            dma((EARLY,)),
            VMEM((rows, LANES), jnp.float32),
            VMEM((rows, LANES), jnp.float32),
            VMEM((8, LANES), jnp.float32),
            VMEM((count, 8, LANES), jnp.float32),
            VMEM((8, LANES), jnp.int32),
            VMEM((count, 8, LANES), jnp.int32),
            dma((steps,)),
            dma((2, count)),
            dma((2, count)),
        ],
        compiler_params=comm_params(1),
    )(block_cols[None, :], teacher_logits, student_logits)

    cols = all_cols[:, 0, :MAXB].reshape(count, count, per_dest)
    cols = lax.dynamic_index_in_dim(cols, me, 1, keepdims=False).reshape(MAXB)
    tile = cols // 2
    first = jnp.argmax(tile[:, None] == tile[None, :], axis=1).astype(jnp.int32)
    place = jnp.clip(ids, 0, width - 1) // LANES
    sides = (lax.iota(jnp.int32, LANES)[None, :] // BLK == (cols % 2)[:, None]).astype(jnp.float32)

    whole_tiles = student_logits
    if padded != width:
        whole_tiles = jnp.pad(student_logits, ((0, 0), (0, padded - width)))
    picks, sent_blocks, seen, picked = pl.pallas_call(
        pick_kernel,
        out_shape=(
            b16(MAXB, BLK, rows),
            b16(MAXB, BLK // 2, LANES),
            b16(MAXB, rows, LANES),
            f32(rows, LANES),
        ),
        in_specs=[smem, smem, smem, smem, smem, vmem, any_spec, vmem, any_spec],
        out_specs=(vmem, vmem, vmem, vmem),
        scratch_shapes=[
            VMEM(teacher_logits.shape, jnp.bfloat16),
            VMEM((rows, ROWS, LANES), jnp.bfloat16),
            VMEM((MAXB, BLK, rows), jnp.float32),
            VMEM((MAXB * BLK // 2, LANES), jnp.float32),
            dma,
            dma((MAXB,)),
            dma((rows,)),
        ],
        compiler_params=params(),
    )(block_rows, block_counts, tile, ids, place, align_values, teacher_logits, stats, whole_tiles)

    target, shift, loss = pl.pallas_call(
        functools.partial(loss_kernel, count),
        out_shape=(f32(MAXB, rows, LANES), f32(rows, LANES), f32(1, LANES)),
        in_specs=[vmem, vmem, vmem, vmem, vmem, vmem, vmem, any_spec],
        out_specs=(vmem, vmem, vmem),
        scratch_shapes=[
            VMEM((rows, width), jnp.bfloat16),
            VMEM((rows, LANES), jnp.float32),
            VMEM((rows, LANES), jnp.float32),
            VMEM((8, LANES), jnp.float32),
            VMEM((count, 8, LANES), jnp.float32),
            VMEM((MAXB, BLK, rows), jnp.bfloat16),
            VMEM((MAXB, BLK // 2, LANES), jnp.bfloat16),
            dma((steps,)),
            dma((3, count)),
            dma((3, count)),
        ],
        compiler_params=comm_params(0),
    )(sides, picks, sent_blocks, seen, picked, early_top, early_total, student_logits)
    token_loss = loss.reshape(rows)

    row_spec = pl.BlockSpec((ROWS, 1), lambda i: (i, 0))
    lane_spec = pl.BlockSpec((ROWS, LANES), lambda i: (i, 0))
    wide_spec = pl.BlockSpec((ROWS, padded), lambda i: (i, 0))
    logit_grad = pl.pallas_call(
        grad_kernel,
        out_shape=b16(rows, width),
        grid=(steps,),
        in_specs=[smem, smem, smem, row_spec, lane_spec, vmem, wide_spec],
        out_specs=wide_spec,
        scratch_shapes=[VMEM((MAXB, rows, LANES), jnp.float32)],
        compiler_params=params(),
        cost_estimate=pl.CostEstimate(flops=8 * size, bytes_accessed=4 * size, transcendentals=size),
    )(tile, first, place, ids[:, None], shift, target, student_logits)
    return logit_grad, token_loss


def solution(mesh):
    return jax.shard_map(
        local,
        mesh=mesh,
        in_specs=(
            P(("groups", "tok", "sub"), "vocab"),
            P(("groups", "tok", "sub"), "vocab"),
            P(("groups", "tok", "sub")),
            P("vocab", None),
            P("vocab"),
            P("vocab"),
            P("vocab"),
        ),
        out_specs=(P(("groups", "tok", "sub"), "vocab"), P(("groups", "tok", "sub"))),
        check_vma=False,
    )
```
